768 devices in a mesh: row: 48 (over y_hi, z, core), col: 16 (over x, y_lo).
Axes of the slice: x: 4, y: 8 (y_hi: 2, y_lo: 4; y = y_hi * 4 + y_lo), z: 12, core: 2. Of those that a mesh axis runs over, the one named last changes fastest.
Arguments:
- tile_left: bfloat16 [48, 16, 2048, 128], P('row', 'col'), may hold values from -6 to 6
- tile_right: bfloat16 [48, 16, 2048, 128], P('row', 'col'), may hold values from -1 to 1
- tile_blocks: int32 [48, 16], P('row', 'col'), may hold values from 1 to 4
- panel_left: bfloat16 [2, 48, 2048, 128], P(None, 'row', 'col'), may hold values from -6 to 6
- panel_right: bfloat16 [2, 48, 2048, 128], P(None, 'row', 'col'), may hold values from -2 to 2
- swap_flag: int32 [48, 16], P('row', 'col'), may hold values from 0 to 1, as said below
Outputs:
- grown_left: bfloat16 [48, 16, 2048, 256], P('row', 'col')
- grown_right: bfloat16 [48, 16, 2048, 256], P('row', 'col')
The draws below stay inside these ranges and needn't reach their ends.
Inputs may be any that keep to these rules, and one draw needn't show every extreme that they name: swap_flag[i, c] equals swap_flag[i, (c + 16 / 2) mod 16], so tiles change owner in pairs.
All inputs are finite; a program needn't handle non-finite values.
Results may differ from the reference program's by a relative error of at most 0.0057.
Values may be sent and summed in bfloat16 or wider, within the bound.
No kernel may reach another device: no remote copies, remote signals or barrier semaphores. Data moves between devices by JAX's collectives and lax.ppermute only.
A program may use at most 32 MiB of HBM per device.

```python
import jax
import jax.numpy as jnp
from jax import lax

NB = 2048
RT = 128
RP = 128
RBLK = 32
N_ROW = 48
N_COL = 16


def draw_swap_flag(key, part):
    halves = jax.random.randint(jax.random.fold_in(key, 7), (N_ROW, N_COL // 2), 0, 2)
    return jnp.concatenate([halves, halves], axis=1).astype(jnp.int32)


def draw_panel_right(key, part):
    spread = 0.4 ** 0.5 * (RP * NB) ** (-0.25)
    shape = (2, N_ROW, NB, RP)
    noise = jnp.clip(jax.random.normal(jax.random.fold_in(key, 13), shape, jnp.float32), -6.0, 6.0) * spread
    stride = NB // RP
    rows = lax_rows = jnp.arange(NB, dtype=jnp.int32)
    cols = jnp.arange(RP, dtype=jnp.int32)
    ident = (rows[:, None] == cols[None, :] * stride).astype(jnp.float32)
    return (noise + ident[None, None]).astype(jnp.bfloat16)


def set_ends(array, key, low, largest):
    extent = array.shape
    index_at = [jax.random.randint(jax.random.fold_in(key, axis), (), 0, extent[axis]) for axis in range(len(extent))]
    array = array.at[tuple(index_at)].set(low)
    longest = extent.index(max(extent))
    index_at[longest] = (index_at[longest] + 1) % extent[longest]
    return array.at[tuple(index_at)].set(largest)


def level_of(rng, shape, pieces, low, top_value):
    loudness, own = 1.0, jax.random.fold_in(rng, 6)
    for position, parts in pieces:
        draws = jnp.exp(jax.random.uniform(jax.random.fold_in(own, position), (parts,), jnp.float32, low / len(pieces), top_value / len(pieces)))
        loudness = loudness * jnp.repeat(draws, shape[position] // parts).reshape([-1 if axis == position else 1 for axis in range(len(shape))])
    return loudness


def bell_draw(key, dims, scale, reach, cuts=(), held_as=jnp.bfloat16):
    entries = jax.random.normal(key, dims, jnp.float32) * scale
    if len(cuts) > 0:
        entries = level_of(key, dims, cuts, -0.22, 0.18) * entries
    return jnp.clip(entries, min=-reach, max=reach).astype(held_as)


def setup_inputs(seed: int = 0) -> dict:
    seeds = jax.random.split(jax.random.key(seed), 7)
    return {
        "tile_left": bell_draw(seeds[0], (N_ROW, N_COL, NB, RT), 1.0, 6.0, ((0, 48), (1, 16))),
        "tile_right": bell_draw(seeds[1], (N_ROW, N_COL, NB, RT), ((2 * RT) ** -0.5), 1.0, ((0, 48), (1, 16))),
        "tile_blocks": set_ends(jax.random.randint(seeds[2], (N_ROW, N_COL), 1, RT // RBLK + 1), jax.random.fold_in(seeds[2], 1), 1, (RT // RBLK + 1) - 1).astype(jnp.int32),
        "panel_left": bell_draw(seeds[3], (2, N_ROW, NB, RP), 1.0, 6.0, ((1, 48), (2, 16))),
        "panel_right": draw_panel_right(jax.random.fold_in(seeds[6], 71), 0),
        "swap_flag": draw_swap_flag(jax.random.fold_in(seeds[6], 71), 0),
    }


def expand(row_left, masked_left, masked_right, col_left, coupling, live_cols):
    lifted = (-jnp.dot(row_left.astype(jnp.float32), coupling.astype(jnp.float32), preferred_element_type=jnp.float32)).astype(jnp.bfloat16)
    stacked_left = jnp.concatenate([masked_left, lifted], axis=1)
    stacked_right = jnp.concatenate([masked_right, col_left], axis=1)
    dead_cols = jnp.concatenate([1.0 - live_cols.astype(jnp.float32), jnp.zeros((coupling.shape[1],), jnp.float32)])
    gram_matrix = jnp.dot(stacked_left.T.astype(jnp.float32), stacked_left.astype(jnp.float32), preferred_element_type=jnp.float32) / stacked_left.shape[0]
    gram_matrix = gram_matrix + jnp.diag(dead_cols)
    factor = jnp.linalg.cholesky(gram_matrix)
    left_out = lax.linalg.triangular_solve(factor, stacked_left.astype(jnp.float32), left_side=False, lower=True, transpose_a=True)
    right_out = jnp.dot(stacked_right.astype(jnp.float32), factor, precision=lax.Precision.HIGHEST)
    return (left_out.astype(jnp.bfloat16), right_out.astype(jnp.bfloat16))

def reference(tile_left, tile_right, tile_blocks, panel_left, panel_right, swap_flag):

    def one_tile(flat_index):
        row_index = flat_index // N_COL
        col_index = flat_index % N_COL
        live_mask = jnp.arange(RT, dtype=jnp.int32) < tile_blocks[row_index, col_index] * RBLK
        zero_value = jnp.zeros((), jnp.bfloat16)
        masked_left = jnp.where(live_mask[None, :], tile_left[row_index, col_index], zero_value)
        masked_right = jnp.where(live_mask[None, :], tile_right[row_index, col_index], zero_value)
        coupling = jnp.dot(panel_right[1, row_index].T.astype(jnp.float32), panel_right[0, col_index].astype(jnp.float32), preferred_element_type=jnp.float32).astype(jnp.bfloat16)
        return expand(panel_left[1, row_index], masked_left, masked_right, panel_left[0, col_index], coupling, live_mask.astype(jnp.float32))
    left_all, right_all = lax.map(one_tile, jnp.arange(N_ROW * N_COL, dtype=jnp.int32))
    left_all = left_all.reshape(N_ROW, N_COL, NB, RT + RP)
    right_all = right_all.reshape(N_ROW, N_COL, NB, RT + RP)
    chosen = (swap_flag == 1)[:, :, None, None]
    grown_left = jnp.where(chosen, jnp.roll(left_all, N_COL // 2, axis=1), left_all)
    grown_right = jnp.where(chosen, jnp.roll(right_all, N_COL // 2, axis=1), right_all)
    return (grown_left, grown_right)
```

```python
import jax
import jax.numpy as jnp
from jax import lax
from jax.experimental import pallas as pl
from jax.experimental.pallas import tpu as pltpu
from jax.sharding import PartitionSpec as P

RBLK = 32
NB = 2048
W = 128
NCOL = 16
NROW = 48
HALF = 64
META = 8
NT = (((1,), (1,)), ((), ()))
NN = (((1,), (0,)), ((), ()))
TN = (((0,), (0,)), ((), ()))
F32 = jnp.float32
BF16 = jnp.bfloat16
HIGH = lax.Precision.HIGHEST


def row_at(y_hi, z, core):
    return y_hi * 24 + z * 2 + core


APART = [[row_at(y, p + 4 * g, k) for y in range(2) for g in range(3) for k in range(2)] for p in range(4)]
RUNS = [[row_at(y, 4 * g + p, k) for p in range(4)] for y in range(2) for g in range(3) for k in range(2)]
CORES = [(r, r ^ 1) for r in range(NROW)]
PARTNERS = [(c, c ^ (NCOL // 2)) for c in range(NCOL)]


def sub(x, m):
    return jnp.broadcast_to(x[m : m + 1, :], x.shape)


def lane(x, m):
    return jnp.broadcast_to(x[:, m : m + 1], (8, W))


def cholesky_and_inverse(a):
    n = a.shape[0] // 8
    ri = lax.broadcasted_iota(jnp.int32, (8, W), 0)
    li = lax.broadcasted_iota(jnp.int32, (8, W), 1)
    rows = [a[8 * g : 8 * g + 8, :] for g in range(n)]
    inv_rows = [jnp.where(li == ri + 8 * g, 1.0, 0.0).astype(F32) for g in range(n)]
    upper, inverse = [], []
    for g in range(n):
        k = 8 * g
        ra, rb = rows[g], inv_rows[g]
        diag = [lane(ra, k + m) for m in range(8)]
        below = {h: [lane(rows[h], k + m) for m in range(8)] for h in range(g + 1, n)}
        ua, ub = ra, rb
        scale = jnp.zeros((8, W), F32)
        for m in range(8):
            r = lax.rsqrt(sub(diag[m], m))
            ba, bb = sub(ra, m), sub(rb, m)
            if m:
                ua = jnp.where(ri == m, ba, ua)
                ub = jnp.where(ri == m, bb, ub)
            scale = jnp.where(ri == m, r, scale)
            c = jnp.where(ri == m, 0.0, diag[m] * (r * r))
            for q in range(m + 1, 8):
                diag[q] = diag[q] - c * sub(diag[q], m)
            ra = ra - c * ba
            rb = rb - c * bb
        upper.append(jnp.where(li >= ri + k, ua * scale, 0.0))
        inverse.append(ub * scale)
        if g + 1 < n:
            qa, qb = ra * (scale * scale), rb * (scale * scale)
            sa = [sub(qa, m) for m in range(8)]
            sb = [sub(qb, m) for m in range(8)]
            for h in range(g + 1, n):
                for m in range(8):
                    rows[h] = rows[h] - below[h][m] * sa[m]
                    inv_rows[h] = inv_rows[h] - below[h][m] * sb[m]
    return jnp.concatenate(upper, 0), jnp.concatenate(inverse, 0)


def dot(a, b, dims, precision=None):
    return lax.dot_general(a, b, dims, precision=precision, preferred_element_type=F32)


FLAG, CORE, PLACE_X, PLACE_Y = range(4)
META = 8
OWN = 2 * W + META


def live_count(at, near, far):
    here, there = near[0, 2 * W : OWN, :].astype(F32), far[0, 2 * W : OWN, :].astype(F32)
    return RBLK * jnp.where(at[0, FLAG] == 1, there, here)[:1, :].astype(jnp.int32)


def first_block(at, own0, own2, near, far, masked, factor_t, factor_inv):
    count = live_count(at, own0, own2)
    live = lax.broadcasted_iota(jnp.int32, (NB, W), 1) < count
    u = jnp.where(at[0, FLAG] == 1, far[...].astype(F32), near[...].astype(F32))
    u = jnp.where(live, u, 0.0).astype(BF16)
    masked[...] = u
    gram = dot(u, u, TN) / NB
    ri = lax.broadcasted_iota(jnp.int32, (W, W), 0)
    li = lax.broadcasted_iota(jnp.int32, (W, W), 1)
    gram = gram + jnp.where((ri == li) & (li >= count), 1.0, 0.0)
    upper, inverse = cholesky_and_inverse(gram)
    factor_t[...] = upper
    factor_inv[...] = inverse


def own_rows(at, pieces, first, whole):
    for t in range(4):
        for s in range(4):
            block = ((at[0, PLACE_X] + t) % 4) * 4 + (at[0, PLACE_Y] + s) % 4
            whole[pl.ds(pl.multiple_of(block * W, W), W), :] = pieces[t][s, first : first + W, :]


def column_rows(at, first_half, second_half, whole):
    for core, ref in ((at[0, CORE], first_half), (1 - at[0, CORE], second_half)):
        for p in range(4):
            for q in range(4):
                block = 8 * (q // 2) + 2 * p + q % 2
                start = pl.multiple_of(block * W + core * HALF, HALF)
                whole[pl.ds(start, HALF), :] = ref(p, q)


def couple(at, own0, own1, own2, own3, near, far, coupling, row_right, col_right):
    own_rows(at, (own0, own1, own2, own3), W, row_right)
    column_rows(at, lambda p, q: near[p, q, HALF:], lambda p, q: far[p, q, HALF:], col_right)
    coupling[...] = dot(row_right[...], col_right[...], TN).astype(BF16)


def parts(x):
    high = x.astype(BF16)
    return high, (x - high.astype(F32)).astype(BF16)


def second_block(
    at, own0, own1, own2, own3, near, far, masked, factor_t, factor_inv, left_out, factor, row_left
):
    own_rows(at, (own0, own1, own2, own3), 0, row_left)
    coupling = jnp.where(at[0, FLAG] == 1, far[...].astype(F32), near[...].astype(F32)).astype(BF16)
    up = (-dot(row_left[...], coupling, NN)).astype(BF16)
    u = masked[...]
    inv11 = factor_inv[...]
    f11t = factor_t[...]
    g12 = dot(u, up, TN) / NB
    g22 = dot(up, up, TN) / NB
    f21t = dot(inv11, g12, NN, HIGH)
    f22t, inv22 = cholesky_and_inverse(g22 - dot(f21t, f21t, TN, HIGH))
    inv21 = -dot(inv22, dot(f21t, inv11, TN, HIGH), NN, HIGH)
    zero = jnp.zeros((W, W), F32)
    factor[...] = jnp.concatenate(
        [jnp.concatenate([f11t, f21t], 1), jnp.concatenate([zero, f22t], 1)], 0
    )
    inverse = jnp.concatenate(
        [jnp.concatenate([inv11, zero], 1), jnp.concatenate([inv21, inv22], 1)], 0
    )
    high, low = parts(inverse)
    row_left[...] = up
    for first in range(0, NB, 512):
        here = pl.ds(first, 512)
        s = jnp.concatenate([masked[here, :], row_left[here, :]], 1)
        left_out[here, :] = (dot(s, high, NT) + dot(s, low, NT)).astype(BF16)


def third_block(
    at, own0, own2, near_right, far_right, near, far, near_swapped, far_swapped, factor, right_out,
    col_left,
):
    flag = at[0, FLAG]

    def either(swapped, kept):
        def read(p, q):
            a, b = swapped[p, q].astype(F32), kept[p, q, :HALF].astype(F32)
            return jnp.where(flag == 1, a, b).astype(BF16)

        return read

    column_rows(at, either(near_swapped, near), either(far_swapped, far), col_left)
    high, low = parts(factor[...])
    live = lax.broadcasted_iota(jnp.int32, (512, W), 1) < live_count(at, own0, own2)
    for first in range(0, NB, 512):
        here = pl.ds(first, 512)
        v = jnp.where(flag == 1, far_right[here, :].astype(F32), near_right[here, :].astype(F32))
        v = jnp.where(live, v, 0.0).astype(BF16)
        t = jnp.concatenate([v, col_left[here, :]], 1)
        right_out[here, :] = (dot(t, high, NT) + dot(t, low, NT)).astype(BF16)


VMEM = pl.BlockSpec(memory_space=pltpu.VMEM)
SMEM = pl.BlockSpec(memory_space=pltpu.SMEM)


def kernel(body, outs, scratch, megaflops, *args):
    return pl.pallas_call(
        body,
        out_shape=[jax.ShapeDtypeStruct(shape, dtype) for shape, dtype in outs],
        in_specs=[SMEM] + [VMEM] * (len(args) - 1),
        out_specs=[VMEM] * len(outs),
        scratch_shapes=[pltpu.VMEM((NB, W), BF16)] * scratch,
        compiler_params=pltpu.CompilerParams(vmem_limit_bytes=32 * 2**20),
        cost_estimate=pl.CostEstimate(
            flops=megaflops * 10**6, bytes_accessed=2**20, transcendentals=0
        ),
    )(*args)


def to_all(x, size, axis, groups):
    return lax.all_to_all(
        jnp.broadcast_to(x[None], (size, *x.shape)).reshape(-1, *x.shape[1:]),
        axis,
        0,
        0,
        tiled=True,
        axis_index_groups=groups,
    )


def per_device(tile_left, tile_right, tile_blocks, panel_left, panel_right, swap_flag):
    row = lax.axis_index("row")
    col = lax.axis_index("col")
    core = row % 2

    blocks = jnp.concatenate(
        [panel_left[0].reshape(2, HALF, W), panel_right[0].reshape(2, HALF, W)], axis=1
    )
    turned = lax.ppermute(
        blocks, ("row", "col"), [(j * NCOL + c, c * NCOL + j) for j in range(NCOL) for c in range(NCOL)]
    )

    counts = jnp.broadcast_to(tile_blocks.astype(BF16), (META, W))
    held = jnp.concatenate([panel_left[1, 0], panel_right[1, 0], counts], 0)
    along_y = [held]
    for s in range(1, 4):
        along_y.append(
            lax.ppermute(held, "col", [(4 * (c // 4) + (c + s) % 4, c) for c in range(NCOL)])
        )
    own = [jnp.stack(along_y)]
    for t in range(1, 4):
        own.append(lax.ppermute(own[0], "col", [((c + 4 * t) % NCOL, c) for c in range(NCOL)]))
    tile_left, tile_right = tile_left[0, 0], tile_right[0, 0]
    tile_left_far = lax.ppermute(tile_left, "col", PARTNERS)
    tile_right_far = lax.ppermute(tile_right, "col", PARTNERS)
    at = jnp.stack([swap_flag[0, 0], core, col // 4, col % 4]).astype(jnp.int32).reshape(1, 4)
    square = ((W, W), F32)
    masked, factor_t, factor_inv = kernel(
        first_block, [((NB, W), BF16), square, square], 0, 6000,
        at, own[0], own[2], tile_left, tile_left_far,
    )

    piece = to_all(turned, 6, "row", APART)[:4]
    piece, own = lax.optimization_barrier((piece, own))
    near = to_all(piece[None], 4, "row", RUNS).reshape(4, 4, W, W)
    near, factor_inv, tile_right_far = lax.optimization_barrier((near, factor_inv, tile_right_far))
    far = lax.ppermute(near, "row", CORES)
    near_swapped = lax.ppermute(near[:, :, :HALF], "col", PARTNERS)
    far_swapped = lax.ppermute(near_swapped, "row", CORES)

    (coupling,) = kernel(couple, [((W, W), BF16)], 2, 2000, at, *own, near, far)
    coupling_far = lax.ppermute(coupling, "col", PARTNERS)
    left_out, factor = kernel(
        second_block, [((NB, 2 * W), BF16), ((2 * W, 2 * W), F32)], 1, 8000,
        at, *own, coupling, coupling_far, masked, factor_t, factor_inv,
    )
    (right_out,) = kernel(
        third_block, [((NB, 2 * W), BF16)], 1, 2000,
        at, own[0], own[2], tile_right, tile_right_far, near, far, near_swapped, far_swapped, factor,
    )
    return left_out[None, None], right_out[None, None]


def solution(mesh):
    placed = (
        P("row", "col", None, None),
        P("row", "col", None, None),
        P("row", "col"),
        P(None, "row", "col", None),
        P(None, "row", "col", None),
        P("row", "col"),
    )
    return jax.shard_map(
        per_device,
        mesh=mesh,
        in_specs=placed,
        out_specs=(P("row", "col", None, None), P("row", "col", None, None)),
        check_vma=False,
    )
```

```python
import jax
import jax.numpy as jnp
from jax import lax
from jax.experimental import pallas as pl
from jax.experimental.pallas import tpu as pltpu
from jax.sharding import PartitionSpec as P

RBLK = 32
NB = 2048
W = 128
NCOL = 16
NROW = 48
HALF = 64
META = 8
NT = (((1,), (1,)), ((), ()))
NN = (((1,), (0,)), ((), ()))
TN = (((0,), (0,)), ((), ()))
F32 = jnp.float32
BF16 = jnp.bfloat16
HIGH = lax.Precision.HIGHEST


def row_at(y_hi, z, core):
    return y_hi * 24 + z * 2 + core


CORES = [(r, r ^ 1) for r in range(NROW)]
PARTNERS = [(c, c ^ (NCOL // 2)) for c in range(NCOL)]


def sub(x, m):
    return jnp.broadcast_to(x[m : m + 1, :], x.shape)


def lane(x, m):
    return jnp.broadcast_to(x[:, m : m + 1], (8, W))


def cholesky_and_inverse(a):
    n = a.shape[0] // 8
    ri = lax.broadcasted_iota(jnp.int32, (8, W), 0)
    li = lax.broadcasted_iota(jnp.int32, (8, W), 1)
    rows = [a[8 * g : 8 * g + 8, :] for g in range(n)]
    inv_rows = [jnp.where(li == ri + 8 * g, 1.0, 0.0).astype(F32) for g in range(n)]
    upper, inverse = [], []
    for g in range(n):
        k = 8 * g
        ra, rb = rows[g], inv_rows[g]
        diag = [lane(ra, k + m) for m in range(8)]
        below = {h: [lane(rows[h], k + m) for m in range(8)] for h in range(g + 1, n)}
        ua, ub = ra, rb
        scale = jnp.zeros((8, W), F32)
        for m in range(8):
            r = lax.rsqrt(sub(diag[m], m))
            ba, bb = sub(ra, m), sub(rb, m)
            if m:
                ua = jnp.where(ri == m, ba, ua)
                ub = jnp.where(ri == m, bb, ub)
            scale = jnp.where(ri == m, r, scale)
            c = jnp.where(ri == m, 0.0, diag[m] * (r * r))
            for q in range(m + 1, 8):
                diag[q] = diag[q] - c * sub(diag[q], m)
            ra = ra - c * ba
            rb = rb - c * bb
        upper.append(jnp.where(li >= ri + k, ua * scale, 0.0))
        inverse.append(ub * scale)
        if g + 1 < n:
            qa, qb = ra * (scale * scale), rb * (scale * scale)
            sa = [sub(qa, m) for m in range(8)]
            sb = [sub(qb, m) for m in range(8)]
            for h in range(g + 1, n):
                for m in range(8):
                    rows[h] = rows[h] - below[h][m] * sa[m]
                    inv_rows[h] = inv_rows[h] - below[h][m] * sb[m]
    return jnp.concatenate(upper, 0), jnp.concatenate(inverse, 0)


def dot(a, b, dims, precision=None):
    return lax.dot_general(a, b, dims, precision=precision, preferred_element_type=F32)


FLAG, BLOCKS, CORE, PLACE = range(4)


def first_block(at, tile, out):
    count = at[0, BLOCKS] * RBLK
    live = lax.broadcasted_iota(jnp.int32, (NB, W), 1) < count
    u = jnp.where(live, tile[...].astype(F32), 0.0).astype(BF16)
    gram = dot(u, u, TN) / NB
    ri = lax.broadcasted_iota(jnp.int32, (W, W), 0)
    li = lax.broadcasted_iota(jnp.int32, (W, W), 1)
    gram = gram + jnp.where((ri == li) & (li >= count), 1.0, 0.0)
    upper, inverse = cholesky_and_inverse(gram)
    out[:W, :] = upper
    out[W : 2 * W, :] = inverse
    out[2 * W :, :] = jnp.full((8, W), count, jnp.int32).astype(F32)


def masked(at, near, far, first_near, first_far, here):
    swap = at[0, FLAG] == 1
    count = jnp.where(swap, first_far[2 * W : 2 * W + 1, :], first_near[2 * W : 2 * W + 1, :])
    tile = jnp.where(swap, far[here, :].astype(F32), near[here, :].astype(F32))
    live = lax.broadcasted_iota(jnp.int32, tile.shape, 1).astype(F32) < count
    return jnp.where(live, tile, 0.0).astype(BF16)


def own_rows(own, first):
    return jnp.concatenate([own[c, first : first + W, :] for c in range(NCOL)], 0)


def column_rows(at, first_half, second_half, whole):
    for core, ref in ((at[0, CORE], first_half), (1 - at[0, CORE], second_half)):
        for s in range(4):
            for q in range(4):
                block = 8 * (q // 2) + 2 * ((at[0, PLACE] + s) % 4) + q % 2
                start = pl.multiple_of(block * W + core * HALF, HALF)
                whole[pl.ds(start, HALF), :] = ref(s, q)


def couple(at, own, near, far, coupling, col_right):
    column_rows(at, lambda s, q: near[s, q, HALF:], lambda s, q: far[s, q, HALF:], col_right)
    coupling[...] = dot(own_rows(own, W), col_right[...], TN).astype(BF16)


def parts(x):
    high = x.astype(BF16)
    return high, (x - high.astype(F32)).astype(BF16)


def second_block(
    at, own, near, far, tile_near, tile_far, first_near, first_far, left_out, factor, lifted
):
    swap = at[0, FLAG] == 1
    coupling = jnp.where(swap, far[...].astype(F32), near[...].astype(F32)).astype(BF16)
    up = (-dot(own_rows(own, 0), coupling, NN)).astype(BF16)
    u = masked(at, tile_near, tile_far, first_near, first_far, pl.ds(0, NB))
    f11t = jnp.where(swap, first_far[:W, :], first_near[:W, :])
    inv11 = jnp.where(swap, first_far[W : 2 * W, :], first_near[W : 2 * W, :])
    g12 = dot(u, up, TN) / NB
    g22 = dot(up, up, TN) / NB
    f21t = dot(inv11, g12, NN, HIGH)
    f22t, inv22 = cholesky_and_inverse(g22 - dot(f21t, f21t, TN, HIGH))
    inv21 = -dot(inv22, dot(f21t, inv11, TN, HIGH), NN, HIGH)
    zero = jnp.zeros((W, W), F32)
    factor[...] = jnp.concatenate(
        [jnp.concatenate([f11t, f21t], 1), jnp.concatenate([zero, f22t], 1)], 0
    )
    inverse = jnp.concatenate(
        [jnp.concatenate([inv11, zero], 1), jnp.concatenate([inv21, inv22], 1)], 0
    )
    high, low = parts(inverse)
    lifted[...] = up
    for first in range(0, NB, 512):
        here = pl.ds(first, 512)
        rows = masked(at, tile_near, tile_far, first_near, first_far, here)
        s = jnp.concatenate([rows, lifted[here, :]], 1)
        left_out[here, :] = (dot(s, high, NT) + dot(s, low, NT)).astype(BF16)


def third_block(
    at, tile_near, tile_far, first_near, first_far, near, far, near_swapped, far_swapped, factor,
    right_out, col_left,
):
    flag = at[0, FLAG]

    def either(swapped, kept):
        def read(p, q):
            a, b = swapped[p, q].astype(F32), kept[p, q, :HALF].astype(F32)
            return jnp.where(flag == 1, a, b).astype(BF16)

        return read

    column_rows(at, either(near_swapped, near), either(far_swapped, far), col_left)
    high, low = parts(factor[...])
    for first in range(0, NB, 512):
        here = pl.ds(first, 512)
        v = masked(at, tile_near, tile_far, first_near, first_far, here)
        t = jnp.concatenate([v, col_left[here, :]], 1)
        right_out[here, :] = (dot(t, high, NT) + dot(t, low, NT)).astype(BF16)


VMEM = pl.BlockSpec(memory_space=pltpu.VMEM)
SMEM = pl.BlockSpec(memory_space=pltpu.SMEM)


def kernel(body, outs, scratch, megaflops, *args):
    return pl.pallas_call(
        body,
        out_shape=[jax.ShapeDtypeStruct(shape, dtype) for shape, dtype in outs],
        in_specs=[SMEM] + [VMEM] * (len(args) - 1),
        out_specs=[VMEM] * len(outs),
        scratch_shapes=[pltpu.VMEM((NB, W), BF16)] * scratch,
        compiler_params=pltpu.CompilerParams(vmem_limit_bytes=32 * 2**20),
        cost_estimate=pl.CostEstimate(
            flops=megaflops * 10**6, bytes_accessed=2**20, transcendentals=0
        ),
    )(*args)


def per_device(tile_left, tile_right, tile_blocks, panel_left, panel_right, swap_flag):
    row = lax.axis_index("row")
    col = lax.axis_index("col")
    core = row % 2

    blocks = jnp.concatenate(
        [panel_left[0].reshape(2, HALF, W), panel_right[0].reshape(2, HALF, W)], axis=1
    )
    even = col % 2 == 0
    turned = [
        lax.ppermute(
            jnp.where(even, blocks[k], blocks[1 - k]),
            ("row", "col"),
            [(j * NCOL + c, (c ^ k) * NCOL + j) for j in range(NCOL) for c in range(NCOL)],
        )
        for k in range(2)
    ]
    pair = jnp.where(core == 0, jnp.stack(turned), jnp.stack(turned[::-1]))

    at = jnp.stack([swap_flag[0, 0], tile_blocks[0, 0], core, (row // 2) % 4])
    at = at.astype(jnp.int32).reshape(1, 4)
    tile_left, tile_right = tile_left[0, 0], tile_right[0, 0]
    (first,) = kernel(first_block, [((2 * W + 8, W), F32)], 0, 6000, at, tile_left)
    pair, first = lax.optimization_barrier((pair, first))

    above = lax.ppermute(pair, "row", [(r, r + NROW // 2) for r in range(NCOL)])
    pair = jnp.where(row < NROW // 2, pair, above)
    sent = []
    for t in range(3):
        pairs = [
            (row_at(y, m, k), row_at(y, 4 * ((t + m // 4) % 3) + m % 4, k))
            for y in range(2)
            for m in range(8)
            for k in range(2)
        ]
        sent.append(lax.ppermute(pair, "row", pairs))
    first_far = lax.ppermute(first, "col", PARTNERS)
    tile_left_far = lax.ppermute(tile_left, "col", PARTNERS)
    tile_right_far = lax.ppermute(tile_right, "col", PARTNERS)
    sent, own_parts, first_far, tile_left_far, tile_right_far = lax.optimization_barrier(
        (sent, (panel_left[1, 0], panel_right[1, 0]), first_far, tile_left_far, tile_right_far)
    )
    run = (row % (NROW // 2)) // 8
    piece = jnp.concatenate(
        [
            jnp.where(run == 0, sent[0], jnp.where(run == 1, sent[1], sent[2])),
            jnp.where(run == 0, sent[2], jnp.where(run == 1, sent[0], sent[1])),
        ]
    )

    held = jnp.concatenate(own_parts, 0)
    own = lax.all_to_all(jnp.broadcast_to(held[None], (NCOL, 2 * W, W)), "col", 0, 0, tiled=True)
    near = [piece]
    for s in range(1, 4):
        pairs = [
            (row_at(y, 4 * g + (p + s) % 4, k), row_at(y, 4 * g + p, k))
            for y in range(2)
            for g in range(3)
            for p in range(4)
            for k in range(2)
        ]
        near.append(lax.ppermute(piece, "row", pairs))
    near = jnp.stack(near)
    near, own = lax.optimization_barrier((near, own))
    far = lax.ppermute(near, "row", CORES)
    near_swapped = lax.ppermute(near[:, :, :HALF], "col", PARTNERS)
    far_swapped = lax.ppermute(near_swapped, "row", CORES)

    (coupling,) = kernel(couple, [((W, W), BF16)], 1, 2000, at, own, near, far)
    coupling_far = lax.ppermute(coupling, "col", PARTNERS)
    left_out, factor = kernel(
        second_block, [((NB, 2 * W), BF16), ((2 * W, 2 * W), F32)], 1, 8000,
        at, own, coupling, coupling_far, tile_left, tile_left_far, first, first_far,
    )
    (right_out,) = kernel(
        third_block, [((NB, 2 * W), BF16)], 1, 2000,
        at, tile_right, tile_right_far, first, first_far, near, far, near_swapped, far_swapped, factor,
    )
    return left_out[None, None], right_out[None, None]


def solution(mesh):
    placed = (
        P("row", "col", None, None),
        P("row", "col", None, None),
        P("row", "col"),
        P(None, "row", "col", None),
        P(None, "row", "col", None),
        P("row", "col"),
    )
    return jax.shard_map(
        per_device,
        mesh=mesh,
        in_specs=placed,
        out_specs=(P("row", "col", None, None), P("row", "col", None, None)),
        check_vma=False,
    )
```

```python
import jax
import jax.numpy as jnp
from jax import lax
from jax.experimental import pallas as pl
from jax.experimental.pallas import tpu as pltpu
from jax.sharding import PartitionSpec as P

RBLK = 32
NB = 2048
W = 128
NCOL = 16
NROW = 48
HALF = 64
META = 8
NT = (((1,), (1,)), ((), ()))
NN = (((1,), (0,)), ((), ()))
TN = (((0,), (0,)), ((), ()))
F32 = jnp.float32
BF16 = jnp.bfloat16
HIGH = lax.Precision.HIGHEST


def row_at(y_hi, z, core):
    return y_hi * 24 + z * 2 + core


CORES = [(r, r ^ 1) for r in range(NROW)]
PARTNERS = [(c, c ^ (NCOL // 2)) for c in range(NCOL)]


def sub(x, m):
    return jnp.broadcast_to(x[m : m + 1, :], x.shape)


def lane(x, m):
    return jnp.broadcast_to(x[:, m : m + 1], (8, W))


def cholesky_and_inverse(a):
    n = a.shape[0] // 8
    ri = lax.broadcasted_iota(jnp.int32, (8, W), 0)
    li = lax.broadcasted_iota(jnp.int32, (8, W), 1)
    rows = [a[8 * g : 8 * g + 8, :] for g in range(n)]
    inv_rows = [jnp.where(li == ri + 8 * g, 1.0, 0.0).astype(F32) for g in range(n)]
    upper, inverse = [], []
    for g in range(n):
        k = 8 * g
        ra, rb = rows[g], inv_rows[g]
        diag = [lane(ra, k + m) for m in range(8)]
        below = {h: [lane(rows[h], k + m) for m in range(8)] for h in range(g + 1, n)}
        ua, ub = ra, rb
        scale = jnp.zeros((8, W), F32)
        for m in range(8):
            r = lax.rsqrt(sub(diag[m], m))
            ba, bb = sub(ra, m), sub(rb, m)
            if m:
                ua = jnp.where(ri == m, ba, ua)
                ub = jnp.where(ri == m, bb, ub)
            scale = jnp.where(ri == m, r, scale)
            c = jnp.where(ri == m, 0.0, diag[m] * (r * r))
            for q in range(m + 1, 8):
                diag[q] = diag[q] - c * sub(diag[q], m)
            ra = ra - c * ba
            rb = rb - c * bb
        upper.append(jnp.where(li >= ri + k, ua * scale, 0.0))
        inverse.append(ub * scale)
        if g + 1 < n:
            qa, qb = ra * (scale * scale), rb * (scale * scale)
            sa = [sub(qa, m) for m in range(8)]
            sb = [sub(qb, m) for m in range(8)]
            for h in range(g + 1, n):
                for m in range(8):
                    rows[h] = rows[h] - below[h][m] * sa[m]
                    inv_rows[h] = inv_rows[h] - below[h][m] * sb[m]
    return jnp.concatenate(upper, 0), jnp.concatenate(inverse, 0)


def dot(a, b, dims, precision=None):
    return lax.dot_general(a, b, dims, precision=precision, preferred_element_type=F32)


FLAG, BLOCKS, CORE, PLACE = range(4)


def first_block(at, tile, out):
    count = at[0, BLOCKS] * RBLK
    live = lax.broadcasted_iota(jnp.int32, (NB, W), 1) < count
    u = jnp.where(live, tile[...].astype(F32), 0.0).astype(BF16)
    gram = dot(u, u, TN) / NB
    ri = lax.broadcasted_iota(jnp.int32, (W, W), 0)
    li = lax.broadcasted_iota(jnp.int32, (W, W), 1)
    gram = gram + jnp.where((ri == li) & (li >= count), 1.0, 0.0)
    upper, inverse = cholesky_and_inverse(gram)
    out[:W, :] = upper
    out[W : 2 * W, :] = inverse
    out[2 * W :, :] = jnp.full((8, W), count, jnp.int32).astype(F32)


def masked(at, near, far, first_near, first_far, here):
    swap = at[0, FLAG] == 1
    count = jnp.where(swap, first_far[2 * W : 2 * W + 1, :], first_near[2 * W : 2 * W + 1, :])
    tile = jnp.where(swap, far[here, :].astype(F32), near[here, :].astype(F32))
    live = lax.broadcasted_iota(jnp.int32, tile.shape, 1).astype(F32) < count
    return jnp.where(live, tile, 0.0).astype(BF16)


def own_rows(own, first):
    return jnp.concatenate([own[c, first : first + W, :] for c in range(NCOL)], 0)


def column_rows(at, first_half, second_half, whole):
    for core, ref in ((at[0, CORE], first_half), (1 - at[0, CORE], second_half)):
        for s in range(4):
            for q in range(4):
                block = 8 * (q // 2) + 2 * ((at[0, PLACE] + s) % 4) + q % 2
                start = pl.multiple_of(block * W + core * HALF, HALF)
                whole[pl.ds(start, HALF), :] = ref(s, q)


def couple(at, own, near, far, coupling, col_right):
    column_rows(at, lambda s, q: near[s, q, HALF:], lambda s, q: far[s, q, HALF:], col_right)
    coupling[...] = dot(own_rows(own, W), col_right[...], TN).astype(BF16)


def parts(x):
    high = x.astype(BF16)
    return high, (x - high.astype(F32)).astype(BF16)


def second_block(
    at, own, near, far, tile_near, tile_far, first_near, first_far, left_out, factor, lifted
):
    swap = at[0, FLAG] == 1
    coupling = jnp.where(swap, far[...].astype(F32), near[...].astype(F32)).astype(BF16)
    up = (-dot(own_rows(own, 0), coupling, NN)).astype(BF16)
    u = masked(at, tile_near, tile_far, first_near, first_far, pl.ds(0, NB))
    f11t = jnp.where(swap, first_far[:W, :], first_near[:W, :])
    inv11 = jnp.where(swap, first_far[W : 2 * W, :], first_near[W : 2 * W, :])
    g12 = dot(u, up, TN) / NB
    g22 = dot(up, up, TN) / NB
    f21t = dot(inv11, g12, NN, HIGH)
    f22t, inv22 = cholesky_and_inverse(g22 - dot(f21t, f21t, TN, HIGH))
    inv21 = -dot(inv22, dot(f21t, inv11, TN, HIGH), NN, HIGH)
    zero = jnp.zeros((W, W), F32)
    factor[...] = jnp.concatenate(
        [jnp.concatenate([f11t, f21t], 1), jnp.concatenate([zero, f22t], 1)], 0
    )
    inverse = jnp.concatenate(
        [jnp.concatenate([inv11, zero], 1), jnp.concatenate([inv21, inv22], 1)], 0
    )
    high, low = parts(inverse)
    lifted[...] = up
    for first in range(0, NB, 512):
        here = pl.ds(first, 512)
        rows = masked(at, tile_near, tile_far, first_near, first_far, here)
        s = jnp.concatenate([rows, lifted[here, :]], 1)
        left_out[here, :] = (dot(s, high, NT) + dot(s, low, NT)).astype(BF16)


def third_block(
    at, tile_near, tile_far, first_near, first_far, near, far, near_swapped, far_swapped, factor,
    right_out, col_left,
):
    flag = at[0, FLAG]

    def either(swapped, kept):
        def read(p, q):
            a, b = swapped[p, q].astype(F32), kept[p, q, :HALF].astype(F32)
            return jnp.where(flag == 1, a, b).astype(BF16)

        return read

    column_rows(at, either(near_swapped, near), either(far_swapped, far), col_left)
    high, low = parts(factor[...])
    for first in range(0, NB, 512):
        here = pl.ds(first, 512)
        v = masked(at, tile_near, tile_far, first_near, first_far, here)
        t = jnp.concatenate([v, col_left[here, :]], 1)
        right_out[here, :] = (dot(t, high, NT) + dot(t, low, NT)).astype(BF16)


VMEM = pl.BlockSpec(memory_space=pltpu.VMEM)
SMEM = pl.BlockSpec(memory_space=pltpu.SMEM)


def kernel(body, outs, scratch, megaflops, *args):
    return pl.pallas_call(
        body,
        out_shape=[jax.ShapeDtypeStruct(shape, dtype) for shape, dtype in outs],
        in_specs=[SMEM] + [VMEM] * (len(args) - 1),
        out_specs=[VMEM] * len(outs),
        scratch_shapes=[pltpu.VMEM((NB, W), BF16)] * scratch,
        compiler_params=pltpu.CompilerParams(vmem_limit_bytes=32 * 2**20),
        cost_estimate=pl.CostEstimate(
            flops=megaflops * 10**6, bytes_accessed=2**20, transcendentals=0
        ),
    )(*args)


def per_device(tile_left, tile_right, tile_blocks, panel_left, panel_right, swap_flag):
    row = lax.axis_index("row")
    col = lax.axis_index("col")
    core = row % 2

    blocks = jnp.concatenate(
        [panel_left[0].reshape(2, HALF, W), panel_right[0].reshape(2, HALF, W)], axis=1
    )
    even = col % 2 == 0
    turned = [
        lax.ppermute(
            jnp.where(even, blocks[k], blocks[1 - k]),
            ("row", "col"),
            [(j * NCOL + c, (c ^ k) * NCOL + j) for j in range(NCOL) for c in range(NCOL)],
        )
        for k in range(2)
    ]
    pair = jnp.where(core == 0, jnp.stack(turned), jnp.stack(turned[::-1]))

    at = jnp.stack([swap_flag[0, 0], tile_blocks[0, 0], core, (row // 2) % 4])
    at = at.astype(jnp.int32).reshape(1, 4)
    tile_left, tile_right = tile_left[0, 0], tile_right[0, 0]
    (first,) = kernel(first_block, [((2 * W + 8, W), F32)], 0, 6000, at, tile_left)
    pair, first = lax.optimization_barrier((pair, first))

    above = lax.ppermute(pair, "row", [(r, r + NROW // 2) for r in range(NCOL)])
    pair = jnp.where(row < NROW // 2, pair, above)
    sent = []
    for t in range(3):
        pairs = [
            (row_at(y, m, k), row_at(y, 4 * ((t + m // 4) % 3) + m % 4, k))
            for y in range(2)
            for m in range(8)
            for k in range(2)
        ]
        sent.append(lax.ppermute(pair, "row", pairs))
    first_far = lax.ppermute(first, "col", PARTNERS)
    tile_right_far = lax.ppermute(tile_right, "col", PARTNERS)
    sent, own_parts, tile_swap, first_far, tile_right_far = lax.optimization_barrier(
        (sent, (panel_left[1, 0], panel_right[1, 0]), tile_left, first_far, tile_right_far)
    )
    run = (row % (NROW // 2)) // 8
    piece = jnp.concatenate(
        [
            jnp.where(run == 0, sent[0], jnp.where(run == 1, sent[1], sent[2])),
            jnp.where(run == 0, sent[2], jnp.where(run == 1, sent[0], sent[1])),
        ]
    )

    held = jnp.concatenate(own_parts, 0)
    own = lax.all_to_all(jnp.broadcast_to(held[None], (NCOL, 2 * W, W)), "col", 0, 0, tiled=True)
    tile_left_far = lax.ppermute(tile_swap, "col", PARTNERS)
    near = [piece]
    for s in range(1, 4):
        pairs = [
            (row_at(y, 4 * g + (p + s) % 4, k), row_at(y, 4 * g + p, k))
            for y in range(2)
            for g in range(3)
            for p in range(4)
            for k in range(2)
        ]
        near.append(lax.ppermute(piece, "row", pairs))
    near = jnp.stack(near)
    near, own, tile_left_far = lax.optimization_barrier((near, own, tile_left_far))
    far = lax.ppermute(near, "row", CORES)
    near_swapped = lax.ppermute(near[:, :, :HALF], "col", PARTNERS)
    far_swapped = lax.ppermute(near_swapped, "row", CORES)

    (coupling,) = kernel(couple, [((W, W), BF16)], 1, 2000, at, own, near, far)
    coupling_far = lax.ppermute(coupling, "col", PARTNERS)
    left_out, factor = kernel(
        second_block, [((NB, 2 * W), BF16), ((2 * W, 2 * W), F32)], 1, 8000,
        at, own, coupling, coupling_far, tile_left, tile_left_far, first, first_far,
    )
    (right_out,) = kernel(
        third_block, [((NB, 2 * W), BF16)], 1, 2000,
        at, tile_right, tile_right_far, first, first_far, near, far, near_swapped, far_swapped, factor,
    )
    return left_out[None, None], right_out[None, None]


def solution(mesh):
    placed = (
        P("row", "col", None, None),
        P("row", "col", None, None),
        P("row", "col"),
        P(None, "row", "col", None),
        P(None, "row", "col", None),
        P("row", "col"),
    )
    return jax.shard_map(
        per_device,
        mesh=mesh,
        in_specs=placed,
        out_specs=(P("row", "col", None, None), P("row", "col", None, None)),
        check_vma=False,
    )
```
